512 devices in a mesh: term: 32 (over y, x, core), sector: 16 (over z).
Axes of the slice: x: 4, y: 4, z: 16, core: 2. Of those that a mesh axis runs over, the one named last changes fastest.
Arguments:
- wavefunction: bfloat16 [96, 256, 256], P('sector')
- left_operator_blocks: bfloat16 [384, 256, 256], P('term'), may hold values from -0.01953125 to 0.01953125
- right_operator_blocks: bfloat16 [384, 256, 256], P('term'), may hold values from -0.375 to 0.375
- fetch_index: int32 [32, 16, 16], P('term', 'sector'), may hold values from 0 to 5, as said below
- owner_link: int32 [384, 96], P('term', 'sector'), may hold values from 0 to 15, as said below
- lower_roots: bfloat16 [4, 96, 256, 256], P(None, 'sector', 'term')
- level_shift: float32 [4], replicated, may hold values from 0.5 to 2
Outputs:
- sigma: float32 [96, 256, 256], P('sector', 'term')
- correlations: float32 [4], replicated
The draws below stay inside these ranges and needn't reach their ends.
Inputs may be any that keep to these rules, and one draw needn't show every extreme that they name: `fetch_index`: entry p of every list is a position within the 6 sectors of sector index p. `owner_link`: within the 12 x 6 entries that one device holds, every sector index occurs at least once.
All inputs are finite; a program needn't handle non-finite values.
Results may differ from the reference program's by a relative error of at most 0.0059.
Values may be sent and summed in bfloat16 or wider, within the bound.
A program may use at most 64 MiB of HBM per device.

```python
import math
import jax
import jax.numpy as jnp
from jax import lax

B = 256
SEC_DEV = 6
TERM_DEV = 12
ROOTS = 4
TERM_GROUPS = 32
SECTOR_GROUPS = 16
TERMS = 384
SECTORS = 96


def shared_roots(key):
    return jax.random.normal(key, (ROOTS, SECTORS, B, B), jnp.float32)


def draw_wavefunction(key, part):
    root_vectors = shared_roots(key)
    key = jax.random.fold_in(key, 3)
    noise_key, common_key, sector_key = jax.random.split(key, 3)
    common = jax.random.uniform(common_key, (ROOTS, 1), jnp.float32, -0.5, 0.5)
    spread = jax.random.uniform(sector_key, (ROOTS, SECTORS), jnp.float32, -0.5, 0.5)
    weights = (common + spread)[:, :, None, None]
    noise_part = jax.random.normal(noise_key, (SECTORS, B, B), jnp.float32)
    return (0.8 * noise_part + jnp.sum(weights * root_vectors, axis=0)).astype(jnp.bfloat16)


def draw_lower_roots(key, part):
    root_vectors = shared_roots(key)
    return root_vectors.astype(jnp.bfloat16)


def draw_fetch_index(key, part):
    key = jax.random.fold_in(key, 5)
    return jax.random.randint(key, (TERM_GROUPS, SECTOR_GROUPS, SECTOR_GROUPS), 0, SEC_DEV, jnp.int32)


def draw_owner_link(key, part):
    key = jax.random.fold_in(key, 7)
    link_count = TERM_DEV * SEC_DEV
    extra_key = jax.random.fold_in(key, 1)
    extra_owner = jax.random.randint(extra_key, (TERM_GROUPS * SECTOR_GROUPS, link_count), 0, SECTOR_GROUPS, jnp.int32)
    position = jnp.arange(link_count, dtype=jnp.int32)[None, :]
    owner_base = jnp.where(position < SECTOR_GROUPS, position, extra_owner)
    device_keys = jax.random.split(jax.random.fold_in(key, 2), TERM_GROUPS * SECTOR_GROUPS)
    shuffled = jax.vmap(lambda one_key, one_row: jax.random.permutation(one_key, one_row))(device_keys, owner_base)
    shuffled = shuffled.reshape(TERM_GROUPS, SECTOR_GROUPS, TERM_DEV, SEC_DEV)
    return jnp.transpose(shuffled, (0, 2, 1, 3)).reshape(TERMS, SECTORS).astype(jnp.int32)


def steps_of(key, shape, cuts, smallest, high):
    level = 1.0
    for dim, blocks in cuts:
        steps = jax.random.uniform(jax.random.fold_in(jax.random.fold_in(key, 6), dim), (blocks,), jnp.float32, smallest / len(cuts), high / len(cuts))
        level = level * jnp.repeat(jnp.exp(steps), shape[dim] // blocks).reshape((-1,) + (1,) * (len(shape) - 1 - dim))
    return level


def centred(key, extent, width, limit, cuts=(), kind=jnp.bfloat16):
    result = jax.random.normal(key, extent, jnp.float32) * width
    if len(cuts) > 0:
        result = steps_of(key, extent, cuts, -0.22, 0.18) * result
    return jnp.clip(result, min=-limit, max=limit).astype(kind)


def setup_inputs(seed: int = 0) -> dict:
    seeds = jax.random.split(jax.random.key(seed), 8)
    wavefunction = draw_wavefunction(jax.random.fold_in(seeds[7], 71), 0)
    left_operator_blocks = centred(seeds[1], (TERMS, B, B), (B * TERMS) ** -0.5, 0.01953125, ((0, 32),))
    right_operator_blocks = centred(seeds[2], (TERMS, B, B), B ** -0.5, 0.375, ((0, 32),))
    fetch_index = draw_fetch_index(jax.random.fold_in(seeds[7], 71), 0)
    owner_link = draw_owner_link(jax.random.fold_in(seeds[7], 71), 0)
    lower_roots = draw_lower_roots(jax.random.fold_in(seeds[7], 71), 0)
    level_shift = jnp.clip(jnp.exp(jax.random.uniform(seeds[6], (ROOTS,), jnp.float32, math.log(0.5), math.log(2.0))), 0.5, 2.0)
    return dict(wavefunction=wavefunction, left_operator_blocks=left_operator_blocks, right_operator_blocks=right_operator_blocks, fetch_index=fetch_index, owner_link=owner_link, lower_roots=lower_roots, level_shift=level_shift)


def reference(wavefunction, left_operator_blocks, right_operator_blocks, fetch_index, owner_link, lower_roots, level_shift):
    term_group = jnp.arange(TERMS, dtype=jnp.int32) // TERM_DEV
    left_operator_stack = left_operator_blocks.astype(jnp.float32)
    right_operator_stack = right_operator_blocks.astype(jnp.float32)

    def one_sector(sector):
        owners = owner_link[:, sector]
        fetch_rows = fetch_index[term_group, sector // SEC_DEV]
        position = jnp.take_along_axis(fetch_rows, owners[:, None], axis=1)[:, 0]
        source_sector = (owners * SEC_DEV + position).astype(jnp.int32)
        input_sector_blocks = wavefunction[source_sector].astype(jnp.float32)
        partial_contraction = jnp.einsum("lhm,lmp->lhp", left_operator_stack, input_sector_blocks).astype(jnp.bfloat16)
        partial_contraction = lax.optimization_barrier(partial_contraction).astype(jnp.float32)
        return jnp.einsum("yxz,ysz->xs", partial_contraction, right_operator_stack)

    applied = lax.map(one_sector, jnp.arange(SECTORS, dtype=jnp.int32))
    roots_full = lower_roots.astype(jnp.float32)
    correlations = jnp.sum(roots_full * wavefunction.astype(jnp.float32)[None], axis=(1, 2, 3)) / (SECTORS * B * B)
    sigma = applied + jnp.einsum("k,ksab->sab", level_shift * correlations, roots_full)
    return sigma, correlations
```

```python
import jax
import jax.numpy as jnp
from jax import lax
from jax.experimental import pallas as pl
from jax.experimental.pallas import tpu as pltpu
from jax.sharding import PartitionSpec as P

BF = jnp.bfloat16
F32 = jnp.float32
MESH = pl.DeviceIdType.MESH
NY, NX, NZ = 4, 4, 16
PLANE = 2 * NY * NX
SEC, TERM, B, ROOTS = 6, 12, 256, 4
CELLS = NZ * SEC * B * B
NEAR = 4
SOURCE = {1: 0, 2: 1, 3: 2, 4: 3, 5: 0, 6: 5, 7: 6, 8: 7}
EVENTS = (
    "O0", "F0", "Z1", "P1", "Z5", "Q0", "P5", "Z2", "P2", "C1", "Z6", "P6", "Z3", "P3", "C5",
    "Z7", "P7", "C2", "C6", "Z8", "P8", "Z4", "P4", "C3", "C7", "C8", "C4",
)


def term_of(y, x, c):
    return (y * NX + x) * 2 + c


def kernel(psi_hbm, fetch_v, fetch_s, owner, lb_hbm, rb_hbm, roots_hbm, part_out, corr_out, *scr):
    psi, roots = scr[:2]
    st = (None,) + scr[2:10]
    sb = scr[10:18]
    (blocks, lb, rcat, half, reqv, reqs, corr_buf, corr_mine, part, d2d_s, d2d_r, rs_s, rs_r,
     load_sem, z_send, z_recv, p_send, p_recv, req_send, req_recv, req_local, c_send, c_recv,
     d_send, d_recv, r_send, r_recv) = scr[18:]
    t = lax.axis_index("term")
    z = lax.axis_index("sector")
    y, x, c = t // (2 * NX), (t // 2) % NX, t % 2
    chip = t // 2

    barrier = pltpu.get_barrier_semaphore()
    peers = []
    for dz in range(1, NZ):
        peers.append((t, (z + dz) % NZ))
    for i in range(1, PLANE):
        peers.append(((t + i) % PLANE, z))
    for peer in peers:
        pl.semaphore_signal(barrier, inc=1, device_id=peer, device_id_type=MESH)

    load_psi = pltpu.make_async_copy(psi_hbm, psi, load_sem.at[TERM + 1])
    load_psi.start()
    load_roots = pltpu.make_async_copy(roots_hbm, roots, load_sem.at[TERM + 2])
    load_roots.start()
    load_l = pltpu.make_async_copy(lb_hbm, lb, load_sem.at[TERM])
    load_l.start()
    load_r = []
    for i in range(TERM):
        copy = pltpu.make_async_copy(rb_hbm.at[i], rcat.at[:, pl.ds(i * B, B)], load_sem.at[i])
        copy.start()
        load_r.append(copy)

    reqv[t] = jnp.zeros((1, 128), jnp.int32)
    reqv[t, :, 0:NZ] = fetch_v[...]

    pl.semaphore_wait(barrier, len(peers))

    def remote(src, dst, send, recv, peer):
        return pltpu.make_async_remote_copy(
            src, dst, send, recv, device_id=peer, device_id_type=MESH
        )

    def wait_bytes(ref, sem):
        pltpu.make_async_copy(ref, ref, sem).wait()

    def quarter(k):
        return jnp.where((z + k + c) % 2 == 0, y, x)

    col = pl.multiple_of(c * 128, 128)

    def z_copy(k, d, h, src_k):
        hop = k - src_k
        peer = (t, (z + (hop if d == 0 else NZ - hop)) % NZ)
        sl = pl.ds(h * 3, 3)
        own = quarter(src_k) * 64 if k <= NEAR else chip * 16
        own = pl.ds(pl.multiple_of(own, 16), 64 if k <= NEAR else 16)
        if src_k == 0:
            src = psi.at[sl, own, pl.ds(col, 128)]
        else:
            src = st[src_k].at[d, sl]
        dst = st[k].at[d, sl] if k < 8 else st[k].at[0, sl]
        n = ((k - 1) * 2 + d) * 2 + h
        return remote(src, dst, z_send.at[n], z_recv.at[n], peer)

    def halves(k, d):
        return (0, 1) if k < 8 else (d,)

    def z_start(k, d):
        for h in halves(k, d):
            z_copy(k, d, h, SOURCE[k]).start()

    def z_event(k):
        for h in (0, 1):
            for d in (0, 1):
                if h in halves(k, d):
                    z_copy(k, d, h, SOURCE[k]).wait_recv()
                for later in range(k + 1, 9):
                    if SOURCE[later] == k and h in halves(later, d):
                        z_copy(later, d, h, k).start()

    def dirs(k):
        return 1 if k == 8 else 2

    def select(k, peer, store):
        for d in range(dirs(k)):
            p = (z + (NZ - k if d == 0 else k)) % NZ
            store(d, st[k][d, reqs[peer, 0, p]])

    def p_event(k):
        if k <= NEAR:
            start, size = quarter(k) * 64, 64
        else:
            start, size = chip * 16, 16
        rows = pl.ds(pl.multiple_of(start, 16), size)
        dst = blocks.at[k - 1, 0:dirs(k), c, rows, :]

        def keep(d, piece):
            blocks[k - 1, d, c, rows, :] = piece

        def send(n, peer):
            def stage(d, piece):
                sb[k - 1][n, d] = piece

            select(k, peer, stage)
            remote(sb[k - 1].at[n], dst, p_send.at[k - 1], p_recv.at[k - 1], (peer, z)).start()

        select(k, t, keep)
        if k <= NEAR:
            even = (z + k + c) % 2 == 0
            for n in range(1, 8):
                dq, dc = n // 2, n % 2
                yy = jnp.where(even, (y + dq) % NY, y)
                xx = jnp.where(even, x, (x + dq) % NX)
                send(n - 1, term_of(yy, xx, (c + dc) % 2))
        else:
            @pl.loop(1, PLANE)
            def _(i):
                send(i - 1, lax.rem(t + i, PLANE))

    def p_whole(k):
        return sb[k - 1]

    def first_products(rel, block):
        half[rel] = jnp.dot(lb[...], block, preferred_element_type=F32).astype(BF)

    def c_event(k):
        wait_bytes(p_whole(k), p_recv.at[k - 1])
        for d in range(dirs(k)):
            block = jnp.concatenate([blocks[k - 1, d, 0], blocks[k - 1, d, 1]], axis=1)
            first_products(NZ - k if d == 0 else k, block)

    groups = (
        (t, [((t + i) % PLANE, z) for i in range(1, PLANE)]),
        (z, [(t, (z + i) % NZ) for i in range(1, NZ)]),
    )

    def q_start(g):
        slot, others = groups[g]
        corr_buf[g, slot] = corr_mine[g]
        for peer in others:
            remote(corr_mine.at[g], corr_buf.at[g, slot], c_send.at[g], c_recv.at[g], peer).start()

    def q_event(g):
        n = len(groups[g][1])
        wait_bytes(corr_buf.at[g, pl.ds(0, n)], c_recv.at[g])
        total = corr_buf[g, 0]
        for i in range(1, n + 1):
            total = total + corr_buf[g, i]
        corr_mine[g + 1] = total
        if g + 1 < len(groups):
            q_start(g + 1)

    for i in range(1, PLANE):
        remote(reqv.at[t], reqv.at[t], req_send, req_recv, ((t + i) % PLANE, z)).start()
    load_psi.wait()
    for d in (0, 1):
        for k in range(1, 9):
            if SOURCE[k] == 0:
                z_start(k, d)
    load_roots.wait()
    rows16 = psi[:, pl.ds(pl.multiple_of(chip * 16, 16), 16), :].astype(F32)
    mine = jnp.where(c == 0, rows16[:, :8, :], rows16[:, 8:, :])
    lines = []
    for k in range(ROOTS):
        prod = jnp.sum(roots[k].astype(F32) * mine, axis=0)
        prod = prod[:, :128] + prod[:, 128:]
        lines.append(jnp.sum(prod, axis=0, keepdims=True))
    corr_mine[0] = jnp.concatenate(lines + [jnp.zeros((8 - ROOTS, 128), F32)], axis=0)
    q_start(0)

    def own_event(_):
        load_l.wait()
        first_products(0, psi[fetch_s[0, z]])

    def f_event(_):
        wait_bytes(reqv.at[pl.ds(0, PLANE - 1)], req_recv)
        to_scalars = pltpu.make_async_copy(reqv, reqs, req_local)
        to_scalars.start()
        to_scalars.wait()

    for event in EVENTS:
        arg = int(event[1:])
        {
            "Z": z_event, "P": p_event, "C": c_event, "Q": q_event, "F": f_event, "O": own_event,
        }[event[0]](arg)

    for copy in load_r:
        copy.wait()

    def sector_sum(s):
        def place(i):
            return (owner[s, i] + NZ - z) % NZ

        total = None
        for g in range(0, TERM, 4):
            lhs = jnp.concatenate([half[place(i), pl.ds(i * B, B)] for i in range(g, g + 4)], axis=1)
            prod = lax.dot_general(
                lhs, rcat[:, g * B:(g + 4) * B], (((1,), (1,)), ((), ())), preferred_element_type=F32
            )
            total = prod if total is None else total + prod
        return total.reshape(16, 2, 8, B)

    sibling = (term_of(y, x, 1 - c), z)

    def d2d(u):
        return remote(d2d_s.at[u], d2d_r.at[u], d_send.at[u], d_recv.at[u], sibling)

    def rs_start(u):
        d2d(u).wait_recv()
        total = part[u] + d2d_r[u].astype(F32)
        part[u] = total
        rs_s[u] = total.astype(BF)
        for i in range(1, 16):
            ch = (chip + i) % 16
            remote(rs_s.at[u, ch], rs_r.at[u, chip], r_send.at[u], r_recv.at[u], (ch * 2 + c, z)).start()

    for u in range(3):
        for e in range(2):
            both = sector_sum(2 * u + e)
            keep = jnp.where(c == 0, both[:, 0], both[:, 1])
            give = jnp.where(c == 0, both[:, 1], both[:, 0])
            part[u, :, e * 8:(e + 1) * 8, :] = keep
            d2d_keep = give
            if e == 0:
                part[3, :, 0:8, :] = d2d_keep
            else:
                part[3, :, 8:16, :] = d2d_keep
        d2d_s[u] = part[3].astype(BF)
        d2d(u).start()
        if u > 0:
            rs_start(u - 1)
    rs_start(2)

    q_event(1)
    corr_out[...] = corr_mine[len(groups)]

    for k in range(1, 9):
        for d in (0, 1):
            for h in halves(k, d):
                z_copy(k, d, h, SOURCE[k]).wait_send()
        wait_bytes(p_whole(k), p_send.at[k - 1])
    wait_bytes(reqv.at[pl.ds(0, PLANE - 1)], req_send)
    for g in range(len(groups)):
        wait_bytes(corr_buf.at[g, pl.ds(0, len(groups[g][1]))], c_send.at[g])

    for u in range(3):
        rs_r[u, chip] = jnp.zeros((16, B), BF)
        wait_bytes(rs_s.at[u, pl.ds(0, 15)], r_recv.at[u])
        total = part[u, chip]
        for i in range(16):
            total = total + rs_r[u, i].astype(F32)
        part_out[u] = total
    for u in range(3):
        d2d(u).wait_send()
        wait_bytes(rs_s.at[u, pl.ds(0, 15)], r_send.at[u])


def finish(part, corr_rows, shift, roots, sig, corr_out):
    corr = jnp.sum(corr_rows[...], axis=1, keepdims=True) * (1.0 / CELLS)
    for s in range(SEC):
        out = part[s // 2, s % 2 * 8:s % 2 * 8 + 8]
        for k in range(ROOTS):
            out = out + (corr[k:k + 1] * shift[k]) * roots[k, s].astype(F32)
        sig[s] = out
    for k in range(ROOTS):
        corr_out[k] = jnp.sum(corr[k:k + 1])


def per_device(psi, lb, rb, fetch, owner, roots, shift):
    fetch = fetch.reshape(1, NZ)
    vm = pl.BlockSpec(memory_space=pltpu.VMEM)
    sm = pl.BlockSpec(memory_space=pltpu.SMEM)
    hbm = pl.BlockSpec(memory_space=pl.ANY)
    dma = pltpu.SemaphoreType.DMA
    scratch = [pltpu.VMEM((SEC, B, B), BF), pltpu.VMEM((ROOTS, SEC, 8, B), BF)]
    sizes = [(64 if k <= NEAR else 16, 1 if k == 8 else 2, 7 if k <= NEAR else PLANE - 1) for k in range(1, 9)]
    scratch += [pltpu.VMEM((dirs, SEC, rows, 128), BF) for rows, dirs, _ in sizes]
    scratch += [pltpu.VMEM((count, dirs, rows, 128), BF) for rows, dirs, count in sizes]
    scratch += [
        pltpu.VMEM((8, 2, 2, B, 128), BF),
        pltpu.VMEM((TERM * B, B), BF),
        pltpu.VMEM((B, TERM * B), BF),
        pltpu.VMEM((NZ, TERM * B, B), BF),
        pltpu.VMEM((PLANE, 1, 128), jnp.int32),
        pltpu.SMEM((PLANE, 1, 128), jnp.int32),
        pltpu.VMEM((2, PLANE, 8, 128), F32),
        pltpu.VMEM((3, 8, 128), F32),
        pltpu.VMEM((4, 16, 16, B), F32),
        pltpu.VMEM((3, 16, 16, B), BF),
        pltpu.VMEM((3, 16, 16, B), BF),
        pltpu.VMEM((3, 16, 16, B), BF),
        pltpu.VMEM((3, 16, 16, B), BF),
        dma((TERM + 3,)), dma((32,)), dma((32,)), dma((8,)), dma((8,)),
        dma, dma, dma, dma((2,)), dma((2,)), dma((3,)), dma((3,)), dma((3,)), dma((3,)),
    ]
    part, corr_rows = pl.pallas_call(
        kernel,
        out_shape=(
            jax.ShapeDtypeStruct((3, 16, B), F32),
            jax.ShapeDtypeStruct((8, 128), F32),
        ),
        in_specs=[hbm, vm, sm, sm, hbm, hbm, hbm],
        out_specs=(vm, vm),
        scratch_shapes=scratch,
        compiler_params=pltpu.CompilerParams(
            collective_id=0, has_side_effects=True, vmem_limit_bytes=56 << 20
        ),
    )(psi, fetch, fetch, owner.T, lb.reshape(TERM * B, B), rb, roots)
    return pl.pallas_call(
        finish,
        out_shape=(
            jax.ShapeDtypeStruct((SEC, 8, B), F32),
            jax.ShapeDtypeStruct((ROOTS,), F32),
        ),
        in_specs=[vm, vm, sm, vm],
        out_specs=(vm, sm),
    )(part, corr_rows, shift, roots)


def solution(mesh):
    return jax.shard_map(
        per_device,
        mesh=mesh,
        in_specs=(
            P("sector", None, None),
            P("term", None, None),
            P("term", None, None),
            P("term", "sector", None),
            P("term", "sector"),
            P(None, "sector", "term", None),
            P(),
        ),
        out_specs=(P("sector", "term", None), P()),
        check_vma=False,
    )
```

```python
import jax
import jax.numpy as jnp
from jax import lax
from jax.experimental import pallas as pl
from jax.experimental.pallas import tpu as pltpu
from jax.sharding import PartitionSpec as P

BF = jnp.bfloat16
F32 = jnp.float32
MESH = pl.DeviceIdType.MESH
NY, NX, NZ = 4, 4, 16
PLANE = 2 * NY * NX
SEC, TERM, B, ROOTS = 6, 12, 256, 4
CELLS = NZ * SEC * B * B
NEAR = 4
SOURCE = {1: 0, 2: 1, 3: 2, 4: 3, 5: 0, 6: 5, 7: 6, 8: 7}
EVENTS = (
    "O0", "F0", "Z1", "P1", "Z5", "P5", "Z2", "P2", "C1", "Z6", "P6", "Z3", "P3", "C5", "Z7",
    "P7", "C2", "C6", "Z8", "P8", "Z4", "P4", "C3", "C7", "Q0", "C8", "C4",
)


def term_of(y, x, c):
    return (y * NX + x) * 2 + c


def kernel(psi_hbm, fetch_v, fetch_s, owner, lb_hbm, rb_hbm, roots_hbm, part_out, corr_out, *scr):
    psi, roots = scr[:2]
    st = (None,) + scr[2:10]
    sb = scr[10:18]
    (blocks, lb, rcat, half, reqv, reqs, corr_buf, corr_z, part, d2d_s, d2d_r, rs_s, rs_r,
     load_sem, z_send, z_recv, p_send, p_recv, req_send, req_recv, req_local, c_send, c_recv, qz_send, qz_recv,
     d_send, d_recv, r_send, r_recv) = scr[18:]
    t = lax.axis_index("term")
    z = lax.axis_index("sector")
    y, x, c = t // (2 * NX), (t // 2) % NX, t % 2
    chip = t // 2

    barrier = pltpu.get_barrier_semaphore()
    peers = []
    hops = {k - source for k, source in SOURCE.items()}
    for dz in sorted(hops | {NZ - h for h in hops}):
        peers.append((t, (z + dz) % NZ))
    for i in range(1, PLANE):
        peers.append(((t + i) % PLANE, z))
    for peer in peers:
        pl.semaphore_signal(barrier, inc=1, device_id=peer, device_id_type=MESH)

    load_psi = pltpu.make_async_copy(psi_hbm, psi, load_sem.at[TERM + 1])
    load_psi.start()
    load_roots = pltpu.make_async_copy(roots_hbm, roots, load_sem.at[TERM + 2])
    load_roots.start()
    load_l = pltpu.make_async_copy(lb_hbm, lb, load_sem.at[TERM])
    load_l.start()
    load_r = []
    for i in range(TERM):
        copy = pltpu.make_async_copy(rb_hbm.at[i], rcat.at[:, pl.ds(i * B, B)], load_sem.at[i])
        copy.start()
        load_r.append(copy)

    reqv[t] = jnp.zeros((1, 128), jnp.int32)
    reqv[t, :, 0:NZ] = fetch_v[...]

    pl.semaphore_wait(barrier, len(peers))

    def remote(src, dst, send, recv, peer):
        return pltpu.make_async_remote_copy(
            src, dst, send, recv, device_id=peer, device_id_type=MESH
        )

    def wait_bytes(ref, sem):
        pltpu.make_async_copy(ref, ref, sem).wait()

    def quarter(k):
        return jnp.where((z + k + c) % 2 == 0, y, x)

    col = pl.multiple_of(c * 128, 128)

    def z_copy(k, d, h, src_k):
        hop = k - src_k
        peer = (t, (z + (hop if d == 0 else NZ - hop)) % NZ)
        sl = pl.ds(h * 3, 3)
        own = quarter(src_k) * 64 if k <= NEAR else chip * 16
        own = pl.ds(pl.multiple_of(own, 16), 64 if k <= NEAR else 16)
        if src_k == 0:
            src = psi.at[sl, own, pl.ds(col, 128)]
        else:
            src = st[src_k].at[d, sl]
        dst = st[k].at[d, sl] if k < 8 else st[k].at[0, sl]
        n = ((k - 1) * 2 + d) * 2 + h
        return remote(src, dst, z_send.at[n], z_recv.at[n], peer)

    def dirs(k):
        return 1 if k == 8 else 2

    def q_copy(k, d, src_k):
        hop = k - src_k
        plane = (z + (NZ - src_k if d == 0 else src_k)) % NZ
        src = corr_z.at[plane]
        peer = (t, (z + (hop if d == 0 else NZ - hop)) % NZ)
        return remote(src, src, qz_send.at[k - 1, d], qz_recv.at[k - 1, d], peer)

    def halves(k, d):
        return (0, 1) if k < 8 else (d,)

    def z_start(k, d):
        for h in halves(k, d):
            z_copy(k, d, h, SOURCE[k]).start()

    def z_event(k):
        for h in (0, 1):
            for d in (0, 1):
                if h in halves(k, d):
                    z_copy(k, d, h, SOURCE[k]).wait_recv()
                for later in range(k + 1, 9):
                    if SOURCE[later] == k and h in halves(later, d):
                        z_copy(later, d, h, k).start()
        for d in range(dirs(k)):
            q_copy(k, d, SOURCE[k]).wait_recv()
            for later in range(k + 1, 9):
                if SOURCE[later] == k and d < dirs(later):
                    q_copy(later, d, k).start()

    def select(k, peer, store):
        for d in range(dirs(k)):
            p = (z + (NZ - k if d == 0 else k)) % NZ
            store(d, st[k][d, reqs[peer, 0, p]])

    def p_event(k):
        if k <= NEAR:
            start, size = quarter(k) * 64, 64
        else:
            start, size = chip * 16, 16
        rows = pl.ds(pl.multiple_of(start, 16), size)
        dst = blocks.at[k - 1, 0:dirs(k), c, rows, :]

        def keep(d, piece):
            blocks[k - 1, d, c, rows, :] = piece

        def send(n, peer):
            def stage(d, piece):
                sb[k - 1][n, d] = piece

            select(k, peer, stage)
            remote(sb[k - 1].at[n], dst, p_send.at[k - 1], p_recv.at[k - 1], (peer, z)).start()

        select(k, t, keep)
        if k <= NEAR:
            even = (z + k + c) % 2 == 0
            for n in range(1, 8):
                dq, dc = n // 2, n % 2
                yy = jnp.where(even, (y + dq) % NY, y)
                xx = jnp.where(even, x, (x + dq) % NX)
                send(n - 1, term_of(yy, xx, (c + dc) % 2))
        else:
            @pl.loop(1, PLANE)
            def _(i):
                send(i - 1, lax.rem(t + i, PLANE))

    def p_whole(k):
        return sb[k - 1]

    def first_products(rel, block):
        half[rel] = jnp.dot(lb[...], block, preferred_element_type=F32).astype(BF)

    def c_event(k):
        wait_bytes(p_whole(k), p_recv.at[k - 1])
        for d in range(dirs(k)):
            block = jnp.concatenate([blocks[k - 1, d, 0], blocks[k - 1, d, 1]], axis=1)
            first_products(NZ - k if d == 0 else k, block)

    def q_event(_):
        total = corr_z[0]
        for i in range(1, NZ):
            total = total + corr_z[i]
        corr_buf[t] = total

        @pl.loop(1, PLANE)
        def _(i):
            remote(corr_buf.at[t], corr_buf.at[t], c_send, c_recv, (lax.rem(t + i, PLANE), z)).start()

    def q_total():
        wait_bytes(corr_buf.at[pl.ds(0, PLANE - 1)], c_recv)
        total = corr_buf[0]
        for i in range(1, PLANE):
            total = total + corr_buf[i]
        return total

    for i in range(1, PLANE):
        remote(reqv.at[t], reqv.at[t], req_send, req_recv, ((t + i) % PLANE, z)).start()
    load_psi.wait()
    for d in (0, 1):
        for k in range(1, 9):
            if SOURCE[k] == 0:
                z_start(k, d)
    load_roots.wait()
    rows16 = psi[:, pl.ds(pl.multiple_of(chip * 16, 16), 16), :].astype(F32)
    mine = jnp.where(c == 0, rows16[:, :8, :], rows16[:, 8:, :])
    lines = []
    for k in range(ROOTS):
        prod = jnp.sum(roots[k].astype(F32) * mine, axis=0)
        prod = prod[:, :128] + prod[:, 128:]
        lines.append(jnp.sum(prod, axis=0, keepdims=True))
    corr_z[z] = jnp.concatenate(lines + [jnp.zeros((8 - ROOTS, 128), F32)], axis=0)
    for k in range(1, 9):
        for d in range(dirs(k)):
            if SOURCE[k] == 0:
                q_copy(k, d, 0).start()

    def own_event(_):
        load_l.wait()
        first_products(0, psi[fetch_s[0, z]])

    def f_event(_):
        wait_bytes(reqv.at[pl.ds(0, PLANE - 1)], req_recv)
        to_scalars = pltpu.make_async_copy(reqv, reqs, req_local)
        to_scalars.start()
        to_scalars.wait()

    for event in EVENTS:
        arg = int(event[1:])
        {
            "Z": z_event, "P": p_event, "C": c_event, "Q": q_event, "F": f_event, "O": own_event,
        }[event[0]](arg)

    for copy in load_r:
        copy.wait()

    def sector_sum(s):
        def place(i):
            return (owner[s, i] + NZ - z) % NZ

        total = None
        for g in range(0, TERM, 4):
            lhs = jnp.concatenate([half[place(i), pl.ds(i * B, B)] for i in range(g, g + 4)], axis=1)
            prod = lax.dot_general(
                lhs, rcat[:, g * B:(g + 4) * B], (((1,), (1,)), ((), ())), preferred_element_type=F32
            )
            total = prod if total is None else total + prod
        return total.reshape(16, 2, 8, B)

    sibling = (term_of(y, x, 1 - c), z)

    def d2d(u):
        return remote(d2d_s.at[u], d2d_r.at[u], d_send.at[u], d_recv.at[u], sibling)

    def rs_start(u):
        d2d(u).wait_recv()
        total = part[u] + d2d_r[u].astype(F32)
        part[u] = total
        rs_s[u] = total.astype(BF)
        for i in range(1, 16):
            ch = (chip + i) % 16
            remote(rs_s.at[u, ch], rs_r.at[u, chip], r_send.at[u], r_recv.at[u], (ch * 2 + c, z)).start()

    for u in range(3):
        for e in range(2):
            both = sector_sum(2 * u + e)
            keep = jnp.where(c == 0, both[:, 0], both[:, 1])
            give = jnp.where(c == 0, both[:, 1], both[:, 0])
            part[u, :, e * 8:(e + 1) * 8, :] = keep
            d2d_keep = give
            if e == 0:
                part[3, :, 0:8, :] = d2d_keep
            else:
                part[3, :, 8:16, :] = d2d_keep
        d2d_s[u] = part[3].astype(BF)
        d2d(u).start()
        if u > 0:
            rs_start(u - 1)
    rs_start(2)

    corr_out[...] = q_total()

    for k in range(1, 9):
        for d in (0, 1):
            for h in halves(k, d):
                z_copy(k, d, h, SOURCE[k]).wait_send()
            if d < dirs(k):
                q_copy(k, d, SOURCE[k]).wait_send()
        wait_bytes(p_whole(k), p_send.at[k - 1])
    wait_bytes(reqv.at[pl.ds(0, PLANE - 1)], req_send)
    wait_bytes(corr_buf.at[pl.ds(0, PLANE - 1)], c_send)

    for u in range(3):
        rs_r[u, chip] = jnp.zeros((16, B), BF)
        wait_bytes(rs_s.at[u, pl.ds(0, 15)], r_recv.at[u])
        total = part[u, chip]
        for i in range(16):
            total = total + rs_r[u, i].astype(F32)
        part_out[u] = total
    for u in range(3):
        d2d(u).wait_send()
        wait_bytes(rs_s.at[u, pl.ds(0, 15)], r_send.at[u])


def finish(part, corr_rows, shift, roots, sig, corr_out):
    corr = jnp.sum(corr_rows[...], axis=1, keepdims=True) * (1.0 / CELLS)
    for s in range(SEC):
        out = part[s // 2, s % 2 * 8:s % 2 * 8 + 8]
        for k in range(ROOTS):
            out = out + (corr[k:k + 1] * shift[k]) * roots[k, s].astype(F32)
        sig[s] = out
    for k in range(ROOTS):
        corr_out[k] = jnp.sum(corr[k:k + 1])


def per_device(psi, lb, rb, fetch, owner, roots, shift):
    fetch = fetch.reshape(1, NZ)
    vm = pl.BlockSpec(memory_space=pltpu.VMEM)
    sm = pl.BlockSpec(memory_space=pltpu.SMEM)
    hbm = pl.BlockSpec(memory_space=pl.ANY)
    dma = pltpu.SemaphoreType.DMA
    scratch = [pltpu.VMEM((SEC, B, B), BF), pltpu.VMEM((ROOTS, SEC, 8, B), BF)]
    sizes = [(64 if k <= NEAR else 16, 1 if k == 8 else 2, 7 if k <= NEAR else PLANE - 1) for k in range(1, 9)]
    scratch += [pltpu.VMEM((dirs, SEC, rows, 128), BF) for rows, dirs, _ in sizes]
    scratch += [pltpu.VMEM((count, dirs, rows, 128), BF) for rows, dirs, count in sizes]
    scratch += [
        pltpu.VMEM((8, 2, 2, B, 128), BF),
        pltpu.VMEM((TERM * B, B), BF),
        pltpu.VMEM((B, TERM * B), BF),
        pltpu.VMEM((NZ, TERM * B, B), BF),
        pltpu.VMEM((PLANE, 1, 128), jnp.int32),
        pltpu.SMEM((PLANE, 1, 128), jnp.int32),
        pltpu.VMEM((PLANE, 8, 128), F32),
        pltpu.VMEM((NZ, 8, 128), F32),
        pltpu.VMEM((4, 16, 16, B), F32),
        pltpu.VMEM((3, 16, 16, B), BF),
        pltpu.VMEM((3, 16, 16, B), BF),
        pltpu.VMEM((3, 16, 16, B), BF),
        pltpu.VMEM((3, 16, 16, B), BF),
        dma((TERM + 3,)), dma((32,)), dma((32,)), dma((8,)), dma((8,)),
        dma, dma, dma, dma, dma, dma((8, 2)), dma((8, 2)), dma((3,)), dma((3,)), dma((3,)), dma((3,)),
    ]
    part, corr_rows = pl.pallas_call(
        kernel,
        out_shape=(
            jax.ShapeDtypeStruct((3, 16, B), F32),
            jax.ShapeDtypeStruct((8, 128), F32),
        ),
        in_specs=[hbm, vm, sm, sm, hbm, hbm, hbm],
        out_specs=(vm, vm),
        scratch_shapes=scratch,
        compiler_params=pltpu.CompilerParams(
            collective_id=0, has_side_effects=True, vmem_limit_bytes=56 << 20
        ),
    )(psi, fetch, fetch, owner.T, lb.reshape(TERM * B, B), rb, roots)
    return pl.pallas_call(
        finish,
        out_shape=(
            jax.ShapeDtypeStruct((SEC, 8, B), F32),
            jax.ShapeDtypeStruct((ROOTS,), F32),
        ),
        in_specs=[vm, vm, sm, vm],
        out_specs=(vm, sm),
    )(part, corr_rows, shift, roots)


def solution(mesh):
    return jax.shard_map(
        per_device,
        mesh=mesh,
        in_specs=(
            P("sector", None, None),
            P("term", None, None),
            P("term", None, None),
            P("term", "sector", None),
            P("term", "sector"),
            P(None, "sector", "term", None),
            P(),
        ),
        out_specs=(P("sector", "term", None), P()),
        check_vma=False,
    )
```

```python
import jax
import jax.numpy as jnp
from jax import lax
from jax.experimental import pallas as pl
from jax.experimental.pallas import tpu as pltpu
from jax.sharding import PartitionSpec as P

BF = jnp.bfloat16
F32 = jnp.float32
MESH = pl.DeviceIdType.MESH
NY, NX, NZ = 4, 4, 16
PLANE = 2 * NY * NX
SEC, TERM, B, ROOTS = 6, 12, 256, 4
CELLS = NZ * SEC * B * B
NEAR = 3
SOURCE = {1: 0, 2: 1, 3: 2, 4: 0, 5: 4, 6: 4, 7: 6, 8: 6}
FAR_FIRST = sorted(
    ((dy, dx) for dy in range(NY) for dx in range(NX) if dy or dx),
    key=lambda o: -min(o[0], NY - o[0]) - min(o[1], NX - o[1]),
)
EVENTS = (
    "O0", "F0", "Z1", "P1", "Z4", "P4", "Z2", "P2", "Z5", "P5", "C1", "Z6", "P6", "C4", "Z3",
    "P3", "Z7", "P7", "C2", "Z8", "P8", "C5", "C6", "Q0", "C3", "C7", "C8",
)


def term_of(y, x, c):
    return (y * NX + x) * 2 + c


def kernel(psi_hbm, fetch_v, fetch_s, owner, lb_hbm, rb_hbm, roots_hbm, part_out, corr_out, *scr):
    psi, roots = scr[:2]
    st = (None,) + scr[2:10]
    sb = scr[10:18]
    (blocks, lb, rcat, half, reqv, reqs, corr_buf, corr_z, part, d2d_s, d2d_r, rs_s, rs_r,
     load_sem, z_send, z_recv, p_send, p_recv, req_send, req_recv, req_local, c_send, c_recv, qz_send, qz_recv,
     d_send, d_recv, r_send, r_recv) = scr[18:]
    t = lax.axis_index("term")
    z = lax.axis_index("sector")
    y, x, c = t // (2 * NX), (t // 2) % NX, t % 2
    chip = t // 2

    barrier = pltpu.get_barrier_semaphore()
    peers = []
    hops = {k - source for k, source in SOURCE.items()}
    for dz in sorted(hops | {NZ - h for h in hops}):
        peers.append((t, (z + dz) % NZ))
    for i in range(1, PLANE):
        peers.append(((t + i) % PLANE, z))
    for peer in peers:
        pl.semaphore_signal(barrier, inc=1, device_id=peer, device_id_type=MESH)

    load_psi = pltpu.make_async_copy(psi_hbm, psi, load_sem.at[TERM + 1])
    load_psi.start()
    load_roots = pltpu.make_async_copy(roots_hbm, roots, load_sem.at[TERM + 2])
    load_roots.start()
    load_l = pltpu.make_async_copy(lb_hbm, lb, load_sem.at[TERM])
    load_l.start()
    load_r = []
    for i in range(TERM):
        copy = pltpu.make_async_copy(rb_hbm.at[i], rcat.at[:, pl.ds(i * B, B)], load_sem.at[i])
        copy.start()
        load_r.append(copy)

    reqv[t] = jnp.zeros((1, 128), jnp.int32)
    reqv[t, :, 0:NZ] = fetch_v[...]

    pl.semaphore_wait(barrier, len(peers))

    def remote(src, dst, send, recv, peer):
        return pltpu.make_async_remote_copy(
            src, dst, send, recv, device_id=peer, device_id_type=MESH
        )

    def wait_bytes(ref, sem):
        pltpu.make_async_copy(ref, ref, sem).wait()

    def quarter(k):
        return jnp.where((z + k + c) % 2 == 0, y, x)

    col = pl.multiple_of(c * 128, 128)

    def z_copy(k, d, h, src_k):
        hop = k - src_k
        peer = (t, (z + (hop if d == 0 else NZ - hop)) % NZ)
        sl = pl.ds(h * 3, 3)
        own = quarter(src_k) * 64 if k <= NEAR else chip * 16
        own = pl.ds(pl.multiple_of(own, 16), 64 if k <= NEAR else 16)
        if src_k == 0:
            src = psi.at[sl, own, pl.ds(col, 128)]
        else:
            src = st[src_k].at[d, sl]
        dst = st[k].at[d, sl] if k < 8 else st[k].at[0, sl]
        n = ((k - 1) * 2 + d) * 2 + h
        return remote(src, dst, z_send.at[n], z_recv.at[n], peer)

    def dirs(k):
        return 1 if k == 8 else 2

    def q_copy(k, d, src_k):
        hop = k - src_k
        plane = (z + (NZ - src_k if d == 0 else src_k)) % NZ
        src = corr_z.at[plane]
        peer = (t, (z + (hop if d == 0 else NZ - hop)) % NZ)
        return remote(src, src, qz_send.at[k - 1, d], qz_recv.at[k - 1, d], peer)

    def halves(k, d):
        return (0, 1) if k < 8 else (d,)

    def z_start(k, d):
        for h in halves(k, d):
            z_copy(k, d, h, SOURCE[k]).start()

    def z_event(k):
        for h in (0, 1):
            for d in (0, 1):
                if h in halves(k, d):
                    z_copy(k, d, h, SOURCE[k]).wait_recv()
                for later in range(k + 1, 9):
                    if SOURCE[later] == k and h in halves(later, d):
                        z_copy(later, d, h, k).start()
        for d in range(dirs(k)):
            q_copy(k, d, SOURCE[k]).wait_recv()
            for later in range(k + 1, 9):
                if SOURCE[later] == k and d < dirs(later):
                    q_copy(later, d, k).start()

    def select(k, peer, store):
        for d in range(dirs(k)):
            p = (z + (NZ - k if d == 0 else k)) % NZ
            store(d, st[k][d, reqs[peer, 0, p]])

    def p_event(k):
        if k <= NEAR:
            start, size = quarter(k) * 64, 64
        else:
            start, size = chip * 16, 16
        rows = pl.ds(pl.multiple_of(start, 16), size)
        dst = blocks.at[k - 1, 0:dirs(k), c, rows, :]

        def keep(d, piece):
            blocks[k - 1, d, c, rows, :] = piece

        def send(n, peer):
            def stage(d, piece):
                sb[k - 1][n, d] = piece

            select(k, peer, stage)
            remote(sb[k - 1].at[n], dst, p_send.at[k - 1], p_recv.at[k - 1], (peer, z)).start()

        select(k, t, keep)
        if k <= NEAR:
            even = (z + k + c) % 2 == 0
            for n in range(1, 8):
                dq, dc = n // 2, n % 2
                yy = jnp.where(even, (y + dq) % NY, y)
                xx = jnp.where(even, x, (x + dq) % NX)
                send(n - 1, term_of(yy, xx, (c + dc) % 2))
        else:
            @pl.loop(1, PLANE)
            def _(i):
                send(i - 1, lax.rem(t + i, PLANE))

    def p_whole(k):
        return sb[k - 1]

    def first_products(rel, block):
        half[rel] = jnp.dot(lb[...], block, preferred_element_type=F32).astype(BF)

    def c_event(k):
        wait_bytes(p_whole(k), p_recv.at[k - 1])
        for d in range(dirs(k)):
            block = jnp.concatenate([blocks[k - 1, d, 0], blocks[k - 1, d, 1]], axis=1)
            first_products(NZ - k if d == 0 else k, block)

    def q_event(_):
        total = corr_z[0]
        for i in range(1, NZ):
            total = total + corr_z[i]
        corr_buf[t] = total

        @pl.loop(1, PLANE)
        def _(i):
            remote(corr_buf.at[t], corr_buf.at[t], c_send, c_recv, (lax.rem(t + i, PLANE), z)).start()

    def q_total():
        wait_bytes(corr_buf.at[pl.ds(0, PLANE - 1)], c_recv)
        total = corr_buf[0]
        for i in range(1, PLANE):
            total = total + corr_buf[i]
        return total

    for i in range(1, PLANE):
        remote(reqv.at[t], reqv.at[t], req_send, req_recv, ((t + i) % PLANE, z)).start()
    load_psi.wait()
    for d in (0, 1):
        for k in range(1, 9):
            if SOURCE[k] == 0:
                z_start(k, d)
    load_roots.wait()
    rows16 = psi[:, pl.ds(pl.multiple_of(chip * 16, 16), 16), :].astype(F32)
    mine = jnp.where(c == 0, rows16[:, :8, :], rows16[:, 8:, :])
    lines = []
    for k in range(ROOTS):
        prod = jnp.sum(roots[k].astype(F32) * mine, axis=0)
        prod = prod[:, :128] + prod[:, 128:]
        lines.append(jnp.sum(prod, axis=0, keepdims=True))
    corr_z[z] = jnp.concatenate(lines + [jnp.zeros((8 - ROOTS, 128), F32)], axis=0)
    for k in range(1, 9):
        for d in range(dirs(k)):
            if SOURCE[k] == 0:
                q_copy(k, d, 0).start()

    def own_event(_):
        load_l.wait()
        first_products(0, psi[fetch_s[0, z]])

    def f_event(_):
        wait_bytes(reqv.at[pl.ds(0, PLANE - 1)], req_recv)
        to_scalars = pltpu.make_async_copy(reqv, reqs, req_local)
        to_scalars.start()
        to_scalars.wait()

    for event in EVENTS:
        arg = int(event[1:])
        {
            "Z": z_event, "P": p_event, "C": c_event, "Q": q_event, "F": f_event, "O": own_event,
        }[event[0]](arg)

    for copy in load_r:
        copy.wait()

    def sector_sum(s):
        def place(i):
            return (owner[s, i] + NZ - z) % NZ

        total = None
        for g in range(0, TERM, 4):
            lhs = jnp.concatenate([half[place(i), pl.ds(i * B, B)] for i in range(g, g + 4)], axis=1)
            prod = lax.dot_general(
                lhs, rcat[:, g * B:(g + 4) * B], (((1,), (1,)), ((), ())), preferred_element_type=F32
            )
            total = prod if total is None else total + prod
        return total.reshape(16, 2, 8, B)

    sibling = (term_of(y, x, 1 - c), z)

    def d2d(u):
        return remote(d2d_s.at[u], d2d_r.at[u], d_send.at[u], d_recv.at[u], sibling)

    def rs_start(u):
        d2d(u).wait_recv()
        total = part[u] + d2d_r[u].astype(F32)
        part[u] = total
        rs_s[u] = total.astype(BF)
        for dy, dx in FAR_FIRST:
            ch = (y + dy) % NY * NX + (x + dx) % NX
            remote(rs_s.at[u, ch], rs_r.at[u, chip], r_send.at[u], r_recv.at[u], (ch * 2 + c, z)).start()

    for u in range(3):
        for e in range(2):
            both = sector_sum(2 * u + e)
            keep = jnp.where(c == 0, both[:, 0], both[:, 1])
            give = jnp.where(c == 0, both[:, 1], both[:, 0])
            part[u, :, e * 8:(e + 1) * 8, :] = keep
            d2d_keep = give
            if e == 0:
                part[3, :, 0:8, :] = d2d_keep
            else:
                part[3, :, 8:16, :] = d2d_keep
        d2d_s[u] = part[3].astype(BF)
        d2d(u).start()
        if u > 0:
            rs_start(u - 1)
    rs_start(2)

    corr_out[...] = q_total()

    for k in range(1, 9):
        for d in (0, 1):
            for h in halves(k, d):
                z_copy(k, d, h, SOURCE[k]).wait_send()
            if d < dirs(k):
                q_copy(k, d, SOURCE[k]).wait_send()
        wait_bytes(p_whole(k), p_send.at[k - 1])
    wait_bytes(reqv.at[pl.ds(0, PLANE - 1)], req_send)
    wait_bytes(corr_buf.at[pl.ds(0, PLANE - 1)], c_send)

    for u in range(3):
        rs_r[u, chip] = jnp.zeros((16, B), BF)
        wait_bytes(rs_s.at[u, pl.ds(0, 15)], r_recv.at[u])
        total = part[u, chip]
        for i in range(16):
            total = total + rs_r[u, i].astype(F32)
        part_out[u] = total
    for u in range(3):
        d2d(u).wait_send()
        wait_bytes(rs_s.at[u, pl.ds(0, 15)], r_send.at[u])


def finish(part, corr_rows, shift, roots, sig, corr_out):
    corr = jnp.sum(corr_rows[...], axis=1, keepdims=True) * (1.0 / CELLS)
    for s in range(SEC):
        out = part[s // 2, s % 2 * 8:s % 2 * 8 + 8]
        for k in range(ROOTS):
            out = out + (corr[k:k + 1] * shift[k]) * roots[k, s].astype(F32)
        sig[s] = out
    for k in range(ROOTS):
        corr_out[k] = jnp.sum(corr[k:k + 1])


def per_device(psi, lb, rb, fetch, owner, roots, shift):
    fetch = fetch.reshape(1, NZ)
    vm = pl.BlockSpec(memory_space=pltpu.VMEM)
    sm = pl.BlockSpec(memory_space=pltpu.SMEM)
    hbm = pl.BlockSpec(memory_space=pl.ANY)
    dma = pltpu.SemaphoreType.DMA
    scratch = [pltpu.VMEM((SEC, B, B), BF), pltpu.VMEM((ROOTS, SEC, 8, B), BF)]
    sizes = [(64 if k <= NEAR else 16, 1 if k == 8 else 2, 7 if k <= NEAR else PLANE - 1) for k in range(1, 9)]
    scratch += [pltpu.VMEM((dirs, SEC, rows, 128), BF) for rows, dirs, _ in sizes]
    scratch += [pltpu.VMEM((count, dirs, rows, 128), BF) for rows, dirs, count in sizes]
    scratch += [
        pltpu.VMEM((8, 2, 2, B, 128), BF),
        pltpu.VMEM((TERM * B, B), BF),
        pltpu.VMEM((B, TERM * B), BF),
        pltpu.VMEM((NZ, TERM * B, B), BF),
        pltpu.VMEM((PLANE, 1, 128), jnp.int32),
        pltpu.SMEM((PLANE, 1, 128), jnp.int32),
        pltpu.VMEM((PLANE, 8, 128), F32),
        pltpu.VMEM((NZ, 8, 128), F32),
        pltpu.VMEM((4, 16, 16, B), F32),
        pltpu.VMEM((3, 16, 16, B), BF),
        pltpu.VMEM((3, 16, 16, B), BF),
        pltpu.VMEM((3, 16, 16, B), BF),
        pltpu.VMEM((3, 16, 16, B), BF),
        dma((TERM + 3,)), dma((32,)), dma((32,)), dma((8,)), dma((8,)),
        dma, dma, dma, dma, dma, dma((8, 2)), dma((8, 2)), dma((3,)), dma((3,)), dma((3,)), dma((3,)),
    ]
    part, corr_rows = pl.pallas_call(
        kernel,
        out_shape=(
            jax.ShapeDtypeStruct((3, 16, B), F32),
            jax.ShapeDtypeStruct((8, 128), F32),
        ),
        in_specs=[hbm, vm, sm, sm, hbm, hbm, hbm],
        out_specs=(vm, vm),
        scratch_shapes=scratch,
        compiler_params=pltpu.CompilerParams(
            collective_id=0, has_side_effects=True, vmem_limit_bytes=56 << 20
        ),
    )(psi, fetch, fetch, owner.T, lb.reshape(TERM * B, B), rb, roots)
    return pl.pallas_call(
        finish,
        out_shape=(
            jax.ShapeDtypeStruct((SEC, 8, B), F32),
            jax.ShapeDtypeStruct((ROOTS,), F32),
        ),
        in_specs=[vm, vm, sm, vm],
        out_specs=(vm, sm),
    )(part, corr_rows, shift, roots)


def solution(mesh):
    return jax.shard_map(
        per_device,
        mesh=mesh,
        in_specs=(
            P("sector", None, None),
            P("term", None, None),
            P("term", None, None),
            P("term", "sector", None),
            P("term", "sector"),
            P(None, "sector", "term", None),
            P(),
        ),
        out_specs=(P("sector", "term", None), P()),
        check_vma=False,
    )
```
